512 devices in a mesh: img: 16 (over z, core), seq: 8 (over y), head: 4 (over x).
Axes of the slice: x: 4, y: 8, z: 8, core: 2. Of those that a mesh axis runs over, the one named last changes fastest.
Arguments:
- queries: bfloat16 [16, 1024, 4096], P('img', 'seq', 'head'), may hold values from -6 to 6
- out_grad: bfloat16 [16, 1024, 4096], P('img', 'seq', 'head'), may hold values from -16 to 16
- text_len: int32 [16], P('img'), may hold values from 256 to 1024, as said below
- image_keys: bfloat16 [32, 1600, 512], P('img', ('seq', 'head')), may hold values from -6 to 6
- image_values: bfloat16 [32, 1600, 512], P('img', ('seq', 'head')), may hold values from -6 to 6
- tile_counts: int32 [16], P('img'), may hold values from 1 to 4, as said below
- tile_slots: int32 [16, 4], P('img'), may hold values from -1 to 31, as said below
- gate_param: float32 [1], replicated, may hold values from 0.3 to 1.5
Outputs:
- query_grad: bfloat16 [16, 1024, 4096], P('img', 'seq', 'head')
- key_grad: bfloat16 [32, 1600, 512], P('img', ('seq', 'head'))
- value_grad: bfloat16 [32, 1600, 512], P('img', ('seq', 'head'))
The draws below stay inside these ranges and needn't reach their ends.
Inputs may be any that keep to these rules, and one draw needn't show every extreme that they name: `tile_counts`: each sample has 1 to 4 tiles, some sample exactly 4; the counts sum to 32. `tile_slots`: entry j of a sample is the slot of its tile j for j below its count and -1 beyond; every slot appears exactly once. `text_len`: some sample has all 1024 positions valid.
All inputs are finite; a program needn't handle non-finite values.
Results may differ from the reference program's by a relative error of at most 0.019.
Values may be sent and summed in bfloat16 or wider, within the bound.
A program may use at most 64 MiB of HBM per device.

```python
import math
import jax
import jax.numpy as jnp
from jax import lax

HEADS = 32
KV_HEADS = 4
HEAD_DIM = 128
TILE_TOK = 1600
MAX_TILES = 4
TEXT_DEV = 128
GROUP = 8
TEXT = 1024
SAMPLES = 16
SLOTS = 32
N_SEQ = 8


def tile_plan(key):
    key = jax.random.fold_in(key, 101)
    first_sample = jax.random.randint(jax.random.fold_in(key, 1), (), 0, SAMPLES)
    counts = jnp.ones((SAMPLES,), jnp.int32).at[first_sample].set(MAX_TILES)

    def add_one(step, current):
        noise_bits = jax.random.randint(jax.random.fold_in(key, step + 2), (SAMPLES,), 0, 1 << 20)
        scores = noise_bits * SAMPLES + jnp.arange(SAMPLES, dtype=jnp.int32)
        scores = jnp.where(current < MAX_TILES, scores, -1)
        chosen = lax.top_k(scores, 1)[1][0]
        return current.at[chosen].add(1)
    counts = lax.fori_loop(0, SLOTS - SAMPLES - MAX_TILES + 1, add_one, counts)
    slot_order = jax.random.permutation(jax.random.fold_in(key, 0), SLOTS).astype(jnp.int32)
    starts = jnp.cumsum(counts) - counts
    tile_index = jnp.arange(MAX_TILES, dtype=jnp.int32)
    where_from = jnp.clip(starts[:, None] + tile_index[None, :], 0, SLOTS - 1)
    slot_table = jnp.where(tile_index[None, :] < counts[:, None], slot_order[where_from], -1)
    return (counts.astype(jnp.int32), slot_table.astype(jnp.int32))


def draw_tile_counts(key, part):
    counts, slot_table = tile_plan(key)
    return counts


def draw_tile_slots(key, part):
    counts, slot_table = tile_plan(key)
    return slot_table


def draw_text_len(key, part):
    key = jax.random.fold_in(key, 5)
    lengths = jax.random.randint(jax.random.fold_in(key, 1), (SAMPLES,), TEXT // 4, TEXT + 1)
    full_sample = jax.random.randint(jax.random.fold_in(key, 2), (), 0, SAMPLES)
    return lengths.at[full_sample].set(TEXT).astype(jnp.int32)


def draw_queries(key, part):
    key = jax.random.fold_in(key, 11)
    array_shape = (SAMPLES, TEXT, HEADS * HEAD_DIM)
    row_scales = jnp.exp(jax.random.uniform(jax.random.fold_in(key, 1), (SAMPLES, TEXT, 1), minval=math.log(0.5), maxval=math.log(2.0)))
    noise_field = jax.random.normal(jax.random.fold_in(key, 2), array_shape, jnp.float32)
    drawn = jnp.clip(noise_field * row_scales, -6.0, 6.0)
    return drawn.astype(jnp.bfloat16)


def draw_image_keys(key, part):
    key = jax.random.fold_in(key, 13)
    array_shape = (SLOTS, TILE_TOK, KV_HEADS * HEAD_DIM)
    row_scales = jnp.exp(jax.random.uniform(jax.random.fold_in(key, 1), (SLOTS, TILE_TOK, 1), minval=math.log(0.3), maxval=math.log(3.0)))
    noise_field = jax.random.normal(jax.random.fold_in(key, 2), array_shape, jnp.float32)
    drawn = jnp.clip(noise_field * row_scales, -6.0, 6.0)
    return drawn.astype(jnp.bfloat16)


def block_levels(stream_key, extent, split, smallest, largest):
    def one(dim, parts):
        draws = jax.random.uniform(jax.random.fold_in(jax.random.fold_in(stream_key, 6), dim), (parts,), jnp.float32, smallest / len(split), largest / len(split))
        return jnp.repeat(jnp.exp(draws), extent[dim] // parts).reshape((-1,) + (1,) * (len(extent) - dim - 1))

    gain = one(*split[0])
    for cut in split[1:]:
        gain = gain * one(*cut)
    return gain


def centred(key, extent, spread, bound, shards=(), kind=jnp.bfloat16):
    values = jax.random.normal(key, extent, jnp.float32) * spread
    if len(shards) > 0:
        values = block_levels(key, extent, shards, -0.22, 0.18) * values
    return jnp.clip(values, min=-bound, max=bound).astype(kind)


def setup_inputs(seed: int = 0) -> dict:
    arg_keys = jax.random.split(jax.random.key(seed), 9)
    return {
        "queries": draw_queries(jax.random.fold_in(arg_keys[8], 71), 0),
        "out_grad": centred(arg_keys[1], (SAMPLES, TEXT, HEADS * HEAD_DIM), 4.0, 16.0, ((0, 16), (1, 8), (2, 4))),
        "text_len": draw_text_len(jax.random.fold_in(arg_keys[8], 71), 0),
        "image_keys": draw_image_keys(jax.random.fold_in(arg_keys[8], 71), 0),
        "image_values": centred(arg_keys[4], (SLOTS, TILE_TOK, KV_HEADS * HEAD_DIM), 1.0, 6.0, ((0, 16), (1, 32))),
        "tile_counts": draw_tile_counts(jax.random.fold_in(arg_keys[8], 71), 0),
        "tile_slots": draw_tile_slots(jax.random.fold_in(arg_keys[8], 71), 0),
        "gate_param": jnp.clip(jax.random.uniform(arg_keys[7], (1,), jnp.float32, 0.3, 1.5), 0.3, 1.5),
    }


def reference(queries, out_grad, text_len, image_keys, image_values, tile_counts, tile_slots, gate_param):
    gate_multiplier = jnp.tanh(gate_param[0])
    score_scale = HEAD_DIM ** -0.5
    positions = jnp.arange(TEXT)
    key_span = MAX_TILES * TILE_TOK

    def one_head(head_args):
        query_rows, grad_rows, key_rows, value_rows, key_mask = head_args
        query_float = query_rows.astype(jnp.float32)
        grad_float = grad_rows.astype(jnp.float32)
        key_float = key_rows.astype(jnp.float32)
        value_float = value_rows.astype(jnp.float32)
        scores = jnp.einsum("rgd,kd->grk", query_float, key_float) * score_scale
        scores = jnp.where(key_mask[None, None, :], scores, -jnp.inf)
        row_max = jnp.max(scores, axis=-1, keepdims=True)
        exponent = jnp.exp(scores - row_max)
        probs = exponent / jnp.sum(exponent, axis=-1, keepdims=True)
        weights = probs.astype(jnp.bfloat16)
        grad_probs = jnp.einsum("rgd,kd->grk", grad_float, value_float)
        delta_rows = jnp.sum(probs * grad_probs, axis=-1, keepdims=True)
        score_grads = (gate_multiplier * probs * (grad_probs - delta_rows) * score_scale).astype(jnp.bfloat16)
        score_float = score_grads.astype(jnp.float32)
        query_grad = jnp.einsum("grk,kd->rgd", score_float, key_float).astype(jnp.bfloat16)
        weight_matrices = weights.astype(jnp.float32).reshape(GROUP, N_SEQ, TEXT_DEV, key_span)
        score_matrices = score_float.reshape(GROUP, N_SEQ, TEXT_DEV, key_span)
        gradient_blocks = grad_float.reshape(N_SEQ, TEXT_DEV, GROUP, HEAD_DIM)
        query_tiles_grouped = query_float.reshape(N_SEQ, TEXT_DEV, GROUP, HEAD_DIM)
        value_contributions = (gate_multiplier * jnp.einsum("luyp,uyln->upn", weight_matrices, gradient_blocks)).astype(jnp.bfloat16)
        key_contributions = jnp.einsum("luyp,uyln->upn", score_matrices, query_tiles_grouped).astype(jnp.bfloat16)
        value_grad = jnp.sum(value_contributions.astype(jnp.float32), axis=0).astype(jnp.bfloat16)
        key_grad = jnp.sum(key_contributions.astype(jnp.float32), axis=0).astype(jnp.bfloat16)
        return query_grad, key_grad, value_grad

    def one_sample(sample_args):
        sample_query, sample_grad, text_length, tile_count, slot_row = sample_args
        usable = jnp.arange(MAX_TILES) < tile_count
        slot_index = jnp.maximum(slot_row, 0).astype(jnp.int32)
        key_mask = jnp.repeat(usable, TILE_TOK)
        row_live = positions < text_length
        grad_live = jnp.where(row_live[:, None], sample_grad, jnp.zeros_like(sample_grad))
        sample_keys = image_keys[slot_index].reshape(key_span, KV_HEADS, HEAD_DIM).transpose(1, 0, 2)
        sample_values = image_values[slot_index].reshape(key_span, KV_HEADS, HEAD_DIM).transpose(1, 0, 2)
        query_heads = sample_query.reshape(TEXT, KV_HEADS, GROUP, HEAD_DIM).transpose(1, 0, 2, 3)
        grad_heads = grad_live.reshape(TEXT, KV_HEADS, GROUP, HEAD_DIM).transpose(1, 0, 2, 3)
        mask_heads = jnp.broadcast_to(key_mask, (KV_HEADS, key_span))
        query_grad, key_grad, value_grad = lax.map(one_head, (query_heads, grad_heads, sample_keys, sample_values, mask_heads))
        query_grad = query_grad.transpose(1, 0, 2, 3).reshape(TEXT, KV_HEADS * GROUP * HEAD_DIM)
        key_grad = key_grad.reshape(KV_HEADS, MAX_TILES, TILE_TOK, HEAD_DIM).transpose(1, 2, 0, 3)
        value_grad = value_grad.reshape(KV_HEADS, MAX_TILES, TILE_TOK, HEAD_DIM).transpose(1, 2, 0, 3)
        key_grad = key_grad.reshape(MAX_TILES, TILE_TOK, KV_HEADS * HEAD_DIM)
        value_grad = value_grad.reshape(MAX_TILES, TILE_TOK, KV_HEADS * HEAD_DIM)
        return query_grad, key_grad, value_grad

    query_grad, key_tiles, value_tiles = lax.map(one_sample, (queries, out_grad, text_len, tile_counts, tile_slots))
    slot_index = jnp.maximum(tile_slots, 0).reshape(-1).astype(jnp.int32)
    usable = (jnp.arange(MAX_TILES)[None, :] < tile_counts[:, None]).reshape(-1)
    key_flat = key_tiles.reshape(SAMPLES * MAX_TILES, TILE_TOK, KV_HEADS * HEAD_DIM).astype(jnp.float32)
    value_flat = value_tiles.reshape(SAMPLES * MAX_TILES, TILE_TOK, KV_HEADS * HEAD_DIM).astype(jnp.float32)
    key_flat = jnp.where(usable[:, None, None], key_flat, jnp.zeros_like(key_flat))
    value_flat = jnp.where(usable[:, None, None], value_flat, jnp.zeros_like(value_flat))
    holder = jnp.zeros((SLOTS, TILE_TOK, KV_HEADS * HEAD_DIM), jnp.float32)
    key_grad = holder.at[slot_index].add(key_flat).astype(jnp.bfloat16)
    value_grad = holder.at[slot_index].add(value_flat).astype(jnp.bfloat16)
    return query_grad, key_grad, value_grad
```

```python
import functools
import math

import jax
import jax.numpy as jnp
from jax import lax
from jax.experimental import pallas as pl
from jax.experimental.pallas import tpu as pltpu
from jax.sharding import PartitionSpec as P

MESH = pl.DeviceIdType.MESH
HEAD_DIM = 128
MAX_TILES = 4
GROUP = 8
CORES = 2
SLOT_DEV = 2
BLOCK = 256
FAR = 1e30


def pad16(n):
    return (n + 15) // 16 * 16


def kernel(
    nx, ny, nz,
    q_ref, g_ref, k_ref, v_ref, len_ref, count_ref, slot_ref, gate_ref,
    dq_ref, dk_ref, dv_ref,
    head_out, head_in, tiles, keys, q_cols, g_cols, q_rows, g_rows,
    row_max, row_sum, row_cross, q_acc, terms, y_out, y_in, own,
    mine, twin, z_out, z_in, back_out, back_in,
    send_sem, recv_sem,
):
    tok = k_ref.shape[1]
    part = nx * tok
    rows = dq_ref.shape[1]
    blocks = GROUP * rows // BLOCK
    scale = HEAD_DIM ** -0.5
    img = lax.axis_index("img")
    y = lax.axis_index("seq")
    x = lax.axis_index("head")
    z, core = img // CORES, img % CORES

    def at_z(t):
        return {"img": lax.rem(z + (t + nz), nz) * CORES + core}

    def at_y(t):
        return {"seq": lax.rem(y + (t + ny), ny)}

    def at_x(t):
        return {"head": lax.rem(x + (t + nx), nx)}

    other_core = {"img": z * CORES + (1 - core)}

    partners = [at_x(t) for t in range(1, nx)] + [other_core]
    for n, at in ((nz, at_z), (ny, at_y)):
        partners += [at(1), at(-1)] if n > 2 else [at(1)]
    barrier = pltpu.get_barrier_semaphore()
    for device in partners:
        pl.semaphore_signal(barrier, inc=1, device_id=device, device_id_type=MESH)

    started = []

    def send(src, dst, device):
        index = len(started)
        copy = pltpu.make_async_remote_copy(
            src_ref=src, dst_ref=dst, send_sem=send_sem.at[index], recv_sem=recv_sem.at[index],
            device_id=device, device_id_type=MESH,
        )
        copy.start()
        started.append(copy)
        return copy

    for h in range(nx):
        for s in range(SLOT_DEV):
            for kv, ref in enumerate((k_ref, v_ref)):
                head_out[h, 2 * s + kv, 0:tok, :] = ref[s, :, h * HEAD_DIM:(h + 1) * HEAD_DIM]
    pl.semaphore_wait(barrier, len(partners))
    arriving = [
        send(head_out.at[lax.rem(x + t, nx)], head_in.at[t], at_x(t)) for t in range(1, nx)
    ]

    positions = y * rows + lax.broadcasted_iota(jnp.int32, (rows, HEAD_DIM), 0)
    live = positions < len_ref[0]
    for g in range(GROUP):
        cut = slice(g * HEAD_DIM, (g + 1) * HEAD_DIM)
        b, r = g * rows // BLOCK, g * rows % BLOCK
        query = q_ref[0, :, cut]
        grad = jnp.where(live, g_ref[0, :, cut], jnp.zeros((rows, HEAD_DIM), jnp.bfloat16))
        q_rows[b, r:r + rows, :] = query
        g_rows[b, r:r + rows, :] = grad
        q_cols[b, :, r:r + rows] = query.T
        g_cols[b, :, r:r + rows] = grad.T
    row_max[...] = jnp.full(row_max.shape, -FAR, jnp.float32)
    row_sum[...] = jnp.zeros(row_sum.shape, jnp.float32)
    row_cross[...] = jnp.zeros(row_cross.shape, jnp.float32)
    q_acc[...] = jnp.zeros(q_acc.shape, jnp.float32)

    for t in range(nx):
        if t > 0:
            arriving[t - 1].wait_recv()
        for q in range(2 * SLOT_DEV):
            block = head_out[x, q, 0:tok, :] if t == 0 else head_in[t, q, 0:tok, :]
            tiles[0, 0, q // 2, q % 2, t * tok:(t + 1) * tok, :] = block

    def gather(n, at, ref, halves, forward=None, work=None):
        half = n // 2
        right = left = None
        if forward is not None:
            forward(0)
        for t in range(1, half + 1):
            if right is not None:
                right.wait_recv()
            if t < half:
                next_right = send(ref(-(t - 1) % n), ref(-t % n), at(1))
            else:
                next_right = send(halves(-(t - 1) % n, 0), halves(half, 0), at(1))
            if left is not None:
                left.wait_recv()
            if t < half:
                next_left = send(ref(t - 1), ref(t), at(-1))
            else:
                next_left = send(halves(t - 1, 1), halves(half, 1), at(-1))
            if forward is not None and t > 1:
                forward(-(t - 1) % n)
                forward(t - 1)
            if work is not None:
                work([0] if t == 1 else [t - 1, -(t - 1) % n])
            right, left = next_right, next_left
        right.wait_recv()
        left.wait_recv()
        if forward is not None:
            forward(half)
        if work is not None:
            work([half])

    twins = []
    gather(
        nz, at_z, lambda d: tiles.at[d, 0], lambda d, p: tiles.at[d, 0, p],
        forward=lambda d: twins.append(send(tiles.at[d, 0], tiles.at[d, 1], other_core)),
    )
    for copy in twins:
        copy.wait_recv()

    for j in range(MAX_TILES):
        slot = jnp.maximum(slot_ref[0, j], 0)
        owner = slot // SLOT_DEV
        step = (owner // CORES + (nz - z)) % nz
        side = (owner + core) % CORES
        for kv in range(2):
            keys[0, kv, j * part:(j + 1) * part, :] = (
                tiles[step, side, slot % SLOT_DEV, kv][0:part]
            )

    bias = [jnp.where(j < count_ref[0], 0.0, FAR).astype(jnp.float32) for j in range(MAX_TILES)]
    to_exp2 = scale * math.log2(math.e)

    def scores_of(c, b):
        scores = jnp.dot(keys[c, 0], q_cols[b], preferred_element_type=jnp.float32) * to_exp2
        grads = jnp.dot(keys[c, 1], g_cols[b], preferred_element_type=jnp.float32)
        return scores, grads

    def tile_rows(j):
        return slice(j * part, (j + 1) * part)

    def first_sweep(chunks):
        def body(i, carry):
            b = i % blocks
            c = chunks[0] if len(chunks) == 1 else jnp.where(i < blocks, chunks[0], chunks[1])
            scores, grads = scores_of(c, b)
            old = row_max[b]
            top = old
            for j in range(MAX_TILES):
                highest = jnp.max(scores[tile_rows(j)], axis=0, keepdims=True)
                top = jnp.maximum(top, highest - bias[j])
            shrink = jnp.exp2(old - top)
            total = row_sum[b] * shrink
            cross = row_cross[b] * shrink
            for j in range(MAX_TILES):
                e = jnp.exp2(scores[tile_rows(j)] - (top + bias[j]))
                total = total + jnp.sum(e, axis=0, keepdims=True)
                cross = cross + jnp.sum(e * grads[tile_rows(j)], axis=0, keepdims=True)
            row_max[b] = top
            row_sum[b] = total
            row_cross[b] = cross
            return carry

        lax.fori_loop(0, len(chunks) * blocks, body, 0)

    gather(
        ny, at_y, lambda d: keys.at[d], lambda d, p: keys.at[d, p], work=first_sweep
    )
    row_max[...] = row_max[...] + jnp.log2(row_sum[...])
    row_cross[...] = row_cross[...] / row_sum[...]

    gate = jnp.tanh(jnp.full((8, HEAD_DIM), gate_ref[0], jnp.float32))[0:1]
    grad_factor = gate * scale

    def second_sweep(chunks):
        for i in range(len(chunks)):
            terms[i] = jnp.zeros(terms.shape[1:], jnp.float32)

        def body(i, carry):
            b = i % blocks
            if len(chunks) == 1:
                c, w = chunks[0], 0
            else:
                c, w = jnp.where(i < blocks, chunks[0], chunks[1]), i // blocks
            scores, grads = scores_of(c, b)
            top, delta = row_max[b], row_cross[b]
            weights, score_grads = [], []
            for j in range(MAX_TILES):
                p = jnp.exp2(scores[tile_rows(j)] - (top + bias[j]))
                weights.append(p)
                score_grads.append(p * (grads[tile_rows(j)] - delta))
            weights = jnp.concatenate(weights, axis=0).astype(jnp.bfloat16)
            score_grads = jnp.concatenate(score_grads, axis=0).astype(jnp.bfloat16)
            terms[w, 0] += jnp.dot(score_grads, q_rows[b], preferred_element_type=jnp.float32)
            terms[w, 1] += jnp.dot(weights, g_rows[b], preferred_element_type=jnp.float32)
            q_acc[b] += lax.dot_general(
                score_grads, keys[c, 0], (((0,), (0,)), ((), ())),
                preferred_element_type=jnp.float32,
            )
            return carry

        lax.fori_loop(0, len(chunks) * blocks, body, 0)

    def scatter(n, at, block, out, arrived, prepare):
        half = n // 2
        right = left = None
        for s in range(half):
            t = half - s
            if s == 0:
                prepare([half])
                out[0, 0, 0] = block(0, half, 0)
                out[1, 0, 1] = block(0, half, 1)
                right = send(out.at[0, 0, 0], arrived.at[0, 0, 0], at(1))
                left = send(out.at[1, 0, 1], arrived.at[1, 0, 1], at(-1))
                continue
            prepare([t, n - t])
            for way in range(2):
                (right, left)[way].wait_recv()
                for p in range(2):
                    value = block(way, (t, n - t)[way], p)
                    if s > 1 or p == way:
                        value = value + arrived[way, s - 1, p]
                    out[way, s, p] = value.astype(out.dtype)
                copy = send(out.at[way, s], arrived.at[way, s], at((1, -1)[way]))
                if way == 0:
                    right = copy
                else:
                    left = copy
        prepare([0])
        right.wait_recv()
        left.wait_recv()
        totals = []
        for p in range(2):
            value = block(0, 0, p)
            for way in range(2):
                if half > 1 or p == way:
                    value = value + arrived[way, half - 1, p]
            totals.append(value)
        return totals

    def y_block(w, d, p):
        value = terms[w, p] * (grad_factor if p == 0 else gate)
        return value

    def y_start(w, d, p):
        return y_block(w, d, p)

    sums = scatter(
        ny, at_y, lambda w, d, p: y_block(w, d, p).astype(jnp.bfloat16)
        if d == ny // 2 else y_block(w, d, p),
        y_out, y_in, second_sweep,
    )
    for kv in range(2):
        for j in range(MAX_TILES):
            own[j, kv, 0:part, :] = sums[kv][j * part:(j + 1) * part].astype(jnp.bfloat16)

    def build(d, side):
        for s in range(SLOT_DEV):
            slot = ((z + d) % nz * CORES + (core + side) % CORES) * SLOT_DEV + s
            which = 0
            found = 0
            for j in range(MAX_TILES):
                hit = jnp.where((slot_ref[0, j] == slot) & (j < count_ref[0]), 1, 0)
                which = which + hit * j
                found = found + hit
            for kv in range(2):
                block = own[which, kv]
                mine[d, side, s, kv] = jnp.where(found > 0, block, jnp.zeros_like(block))

    order = [nz // 2]
    for t in range(nz // 2 - 1, 0, -1):
        order += [t, nz - t]
    order += [0]
    from_twin = {}
    for d in order:
        build(d, 1)
        from_twin[d] = send(mine.at[d, 1], twin.at[d], other_core)
    for d in order:
        build(d, 0)

    for g in range(GROUP):
        b, r = g * rows // BLOCK, g * rows % BLOCK
        dq_ref[0, :, g * HEAD_DIM:(g + 1) * HEAD_DIM] = (
            q_acc[b, r:r + rows, :] * grad_factor
        ).astype(jnp.bfloat16)

    def z_prepare(places):
        for d in places:
            from_twin[d].wait_recv()

    slots = scatter(
        nz, at_z, lambda w, d, p: mine[d, 0, p] + twin[d, p], z_out, z_in, z_prepare
    )

    for s in range(SLOT_DEV):
        for kv in range(2):
            value = slots[s][kv]
            for t in range(nx):
                back_out[t, 2 * s + kv, 0:tok, :] = value[t * tok:(t + 1) * tok]
    returns = [send(back_out.at[t], back_in.at[x], at_x(-t)) for t in range(1, nx)]
    back_in[x] = back_out[0]
    for copy in returns:
        copy.wait_recv()
    for h in range(nx):
        for s in range(SLOT_DEV):
            for kv, ref in enumerate((dk_ref, dv_ref)):
                ref[s, :, h * HEAD_DIM:(h + 1) * HEAD_DIM] = back_in[h, 2 * s + kv, 0:tok, :]
    for copy in started:
        copy.wait_send()


def on_device(mesh_sizes, queries, out_grad, text_len, image_keys, image_values, tile_counts,
              tile_slots, gate_param):
    nx, ny, nz = mesh_sizes
    tok = image_keys.shape[1]
    rows = queries.shape[1]
    part = nx * tok
    pad, tok_pad = pad16(part), pad16(tok)
    span = MAX_TILES * part
    blocks = GROUP * rows // BLOCK
    bf16, f32 = jnp.bfloat16, jnp.float32
    vmem = pl.BlockSpec(memory_space=pltpu.VMEM)
    smem = pl.BlockSpec(memory_space=pltpu.SMEM)
    d = HEAD_DIM
    scratch = [
        ((nx, 2 * SLOT_DEV, tok_pad, d), bf16),
        ((nx, 2 * SLOT_DEV, tok_pad, d), bf16),
        ((nz, CORES, SLOT_DEV, 2, pad, d), bf16),
        ((ny, 2, span, d), bf16),
        ((blocks, d, BLOCK), bf16),
        ((blocks, d, BLOCK), bf16),
        ((blocks, BLOCK, d), bf16),
        ((blocks, BLOCK, d), bf16),
        ((blocks, 1, BLOCK), f32),
        ((blocks, 1, BLOCK), f32),
        ((blocks, 1, BLOCK), f32),
        ((blocks, BLOCK, d), f32),
        ((2, 2, span, d), f32),
        ((2, ny // 2, 2, span, d), bf16),
        ((2, ny // 2, 2, span, d), bf16),
        ((MAX_TILES, 2, pad, d), bf16),
        ((nz, CORES, SLOT_DEV, 2, pad, d), bf16),
        ((nz, SLOT_DEV, 2, pad, d), bf16),
        ((2, nz // 2, SLOT_DEV, 2, pad, d), bf16),
        ((2, nz // 2, SLOT_DEV, 2, pad, d), bf16),
        ((nx, 2 * SLOT_DEV, tok_pad, d), bf16),
        ((nx, 2 * SLOT_DEV, tok_pad, d), bf16),
    ]
    copies = 2 * (nx - 1) + 2 * (ny + ny) + 2 * (nz + nz) + 2 * nz
    return pl.pallas_call(
        functools.partial(kernel, nx, ny, nz),
        out_shape=(
            jax.ShapeDtypeStruct(queries.shape, bf16),
            jax.ShapeDtypeStruct(image_keys.shape, bf16),
            jax.ShapeDtypeStruct(image_values.shape, bf16),
        ),
        in_specs=[vmem, vmem, vmem, vmem, smem, smem, smem, smem],
        out_specs=(vmem, vmem, vmem),
        scratch_shapes=[pltpu.VMEM(shape, dtype) for shape, dtype in scratch] + [
            pltpu.SemaphoreType.DMA((copies,)),
            pltpu.SemaphoreType.DMA((copies,)),
        ],
        compiler_params=pltpu.CompilerParams(
            collective_id=0, has_side_effects=True, vmem_limit_bytes=56 * 1024 * 1024
        ),
        name="cross_attention_backward",
    )(queries, out_grad, image_keys, image_values, text_len, tile_counts, tile_slots, gate_param)


def solution(mesh):
    sizes = (mesh.shape["head"], mesh.shape["seq"], mesh.shape["img"] // CORES)
    return jax.shard_map(
        functools.partial(on_device, sizes),
        mesh=mesh,
        in_specs=(
            P("img", "seq", "head"),
            P("img", "seq", "head"),
            P("img"),
            P("img", ("seq", "head"), None),
            P("img", ("seq", "head"), None),
            P("img"),
            P("img", None),
            P(),
        ),
        out_specs=(
            P("img", "seq", "head"),
            P("img", ("seq", "head"), None),
            P("img", ("seq", "head"), None),
        ),
        check_vma=False,
    )
```

```python
import functools
import math

import jax
import jax.numpy as jnp
from jax import lax
from jax.experimental import pallas as pl
from jax.experimental.pallas import tpu as pltpu
from jax.sharding import PartitionSpec as P

MESH = pl.DeviceIdType.MESH
HEAD_DIM = 128
MAX_TILES = 4
GROUP = 8
CORES = 2
SLOT_DEV = 2
BLOCK = 256
FAR = 1e30


def pad16(n):
    return (n + 15) // 16 * 16


def kernel(
    nx, ny, nz,
    q_hbm, g_hbm, k_hbm, v_hbm, len_ref, count_ref, slot_ref, gate_ref,
    dq_hbm, dk_ref, dv_ref,
    q_ref, g_ref, k_ref, v_ref, dq_ref, head_out, head_in, tiles, keys, rowed,
    stat_out, stat_in, final, terms, q_terms, q_own, y_out, y_in, own,
    mine, twin, z_out, z_in, back_out, back_in,
    send_sem, recv_sem, local_sem,
):
    tok = k_ref.shape[0]
    part = nx * tok
    rows = q_ref.shape[1]
    blocks = GROUP * rows // BLOCK
    scale = HEAD_DIM ** -0.5
    img = lax.axis_index("img")
    y = lax.axis_index("seq")
    x = lax.axis_index("head")
    z, core = img // CORES, img % CORES

    def at_z(t):
        return {"img": lax.rem(z + (t + nz), nz) * CORES + core}

    def at_y(t):
        return {"seq": lax.rem(y + (t + ny), ny)}

    def at_x(t):
        return {"head": lax.rem(x + (t + nx), nx)}

    other_core = {"img": z * CORES + (1 - core)}

    loads = []
    for i, (src, dst) in enumerate(
        ((k_hbm, k_ref), (v_hbm, v_ref), (q_hbm, q_ref), (g_hbm, g_ref))
    ):
        loads.append(pltpu.make_async_copy(src, dst, local_sem.at[i]))
        loads[i].start()

    partners = [at_x(t) for t in range(1, nx)] + [other_core]
    partners += [at_y(t) for t in range(1, ny)]
    partners += [at_z(1), at_z(-1)] if nz > 2 else [at_z(1)]
    barrier = pltpu.get_barrier_semaphore()
    for device in partners:
        pl.semaphore_signal(barrier, inc=1, device_id=device, device_id_type=MESH)

    started = []

    def send(src, dst, device):
        index = len(started)
        copy = pltpu.make_async_remote_copy(
            src_ref=src, dst_ref=dst, send_sem=send_sem.at[index], recv_sem=recv_sem.at[index],
            device_id=device, device_id_type=MESH,
        )
        copy.start()
        started.append(copy)
        return copy

    def run(steps, *rings):
        for _ in range(steps):
            for ring in rings:
                next(ring, None)

    for kv, ref in enumerate((k_ref, v_ref)):
        loads[kv].wait()
        for h in range(nx):
            both = ref[:, :, h * HEAD_DIM:(h + 1) * HEAD_DIM].astype(jnp.float32)
            for s in range(SLOT_DEV):
                head_out[h, 2 * s + kv, 0:tok, :] = both[:, s, :].astype(jnp.bfloat16)
    pl.semaphore_wait(barrier, len(partners))
    arriving = {}
    for t in sorted(range(1, nx), key=lambda t: min(t, nx - t)):
        arriving[t] = send(head_out.at[lax.rem(x + t, nx)], head_in.at[t], at_x(t))

    live = y * rows + lax.broadcasted_iota(jnp.int32, (rows, HEAD_DIM), 0) < len_ref[0]
    loads[2].wait()
    loads[3].wait()
    for g in range(GROUP):
        cut = slice(g * HEAD_DIM, (g + 1) * HEAD_DIM)
        b, r = g * rows // BLOCK, g * rows % BLOCK
        rowed[0, 0, b, r:r + rows, :] = q_ref[0, :, cut]
        rowed[0, 1, b, r:r + rows, :] = jnp.where(
            live, g_ref[0, :, cut], jnp.zeros((rows, HEAD_DIM), jnp.bfloat16)
        )

    def gather(n, at, ref):
        half = n // 2
        copies = {}
        for t in range(1, half + 1):
            for h in range(2):
                for way, step in enumerate((1, -1)):
                    if (way, h) in copies:
                        copies.pop((way, h)).wait_recv()
                    if t < half or h == way:
                        source, target = ref(-step * (t - 1) % n, h), ref(-step * t % n, h)
                        copies[way, h] = send(source, target, at(step))
                yield
        for copy in copies.values():
            copy.wait_recv()
        yield

    def collect():
        for t in range(nx):
            if t > 0:
                arriving[t].wait_recv()
            for q in range(2 * SLOT_DEV):
                block = head_out[x, q, 0:tok, :] if t == 0 else head_in[t, q, 0:tok, :]
                tiles[0, 0, q // 2, q % 2, t * tok:(t + 1) * tok, :] = block

    def gather_z():
        ring = gather(nz, at_z, lambda d, h: tiles.at[d, 0, h])
        twins = []

        def forward(d):
            twins.append(send(tiles.at[d, 0], tiles.at[d, 1], other_core))

        for t in range(1, nz // 2 + 1):
            next(ring)
            next(ring)
            for d in [0] if t == 1 else [t - 1, -(t - 1) % nz]:
                forward(d)
            yield
        next(ring)
        forward(nz // 2)
        yield
        for copy in twins:
            copy.wait_recv()
        for j in range(MAX_TILES):
            slot = jnp.maximum(slot_ref[0, j], 0)
            owner = slot // SLOT_DEV
            step = (owner // CORES + (nz - z)) % nz
            side = (owner + core) % CORES
            for kv in range(2):
                keys[kv, tile_rows(j), :] = tiles[step, side, slot % SLOT_DEV, kv][0:part]
        yield

    bias = [jnp.where(j < count_ref[0], 0.0, FAR).astype(jnp.float32) for j in range(MAX_TILES)]
    to_exp2 = scale * math.log2(math.e)
    by_columns = (((1,), (1,)), ((), ()))

    def scores_of(c, b):
        scores = lax.dot_general(
            keys[0], rowed[c, 0, b], by_columns, preferred_element_type=jnp.float32
        ) * to_exp2
        grads = lax.dot_general(
            keys[1], rowed[c, 1, b], by_columns, preferred_element_type=jnp.float32
        )
        return scores, grads

    def tile_rows(j):
        return slice(j * part, (j + 1) * part)

    def over(chunks, body):
        def step(i, carry):
            if len(chunks) == 1:
                body(chunks[0], 0, i)
            else:
                body(jnp.where(i < blocks, chunks[0], chunks[1]), i // blocks, i % blocks)
            return carry

        lax.fori_loop(0, len(chunks) * blocks, step, 0)

    stats = {}

    def first_sweep(chunks):
        def body(c, w, b):
            scores, grads = scores_of(c, b)
            top = jnp.full((1, BLOCK), -FAR, jnp.float32)
            for j in range(MAX_TILES):
                highest = jnp.max(scores[tile_rows(j)], axis=0, keepdims=True)
                top = jnp.maximum(top, highest - bias[j])
            total = jnp.zeros((1, BLOCK), jnp.float32)
            cross = jnp.zeros((1, BLOCK), jnp.float32)
            for j in range(MAX_TILES):
                e = jnp.exp2(scores[tile_rows(j)] - (top + bias[j]))
                total = total + jnp.sum(e, axis=0, keepdims=True)
                cross = cross + jnp.sum(e * grads[tile_rows(j)], axis=0, keepdims=True)
            stat_out[c, 0, b] = top
            stat_out[c, 1, b] = total
            stat_out[c, 2, b] = cross

        over(chunks, body)
        for d in chunks:
            if d != 0:
                stats[d] = send(stat_out.at[d], stat_in.at[(ny - d) % ny], at_y(d))

    gate = jnp.tanh(jnp.full((8, HEAD_DIM), gate_ref[0], jnp.float32))[0:1]
    grad_factor = gate * scale

    def second_sweep(chunks):
        def body(c, w, b):
            scores, grads = scores_of(c, b)
            top, delta = final[c, 0, b], final[c, 1, b]
            weights, score_grads = [], []
            for j in range(MAX_TILES):
                e = jnp.exp2(scores[tile_rows(j)] - (top + bias[j]))
                weights.append(e)
                score_grads.append(e * (grads[tile_rows(j)] - delta))
            weights = jnp.concatenate(weights, axis=0).astype(jnp.bfloat16)
            score_grads = jnp.concatenate(score_grads, axis=0).astype(jnp.bfloat16)
            terms[0] += jnp.dot(score_grads, rowed[c, 0, b], preferred_element_type=jnp.float32)
            terms[1] += jnp.dot(weights, rowed[c, 1, b], preferred_element_type=jnp.float32)
            q_terms[w, b] = lax.dot_general(
                score_grads, keys[0], (((0,), (0,)), ((), ())),
                preferred_element_type=jnp.float32,
            )

        over(chunks, body)

    def scatter(n, at, block, out, arrived, prepare, finish):
        half = n // 2
        copies = {}

        def total(value, h, step):
            for way in range(2) if step == 0 else [0 if step > 0 else 1]:
                if (way, h) in copies:
                    copies.pop((way, h)).wait_recv()
                    value = value + arrived[way, half - abs(step) - 1, h]
            return value

        for s in range(half):
            t = half - s
            prepare([half] if s == 0 else [t, n - t])
            for h in range(2):
                for way, step in enumerate((1, -1)):
                    if s == 0 and h != way:
                        continue
                    value = block(way if s > 0 else 0, step * t % n, h)
                    out[way, s, h] = total(value, h, step * t).astype(out.dtype)
                    copies[way, h] = send(out.at[way, s, h], arrived.at[way, s, h], at(step))
            yield
        prepare([0])
        for h in range(2):
            finish(h, total(block(0, 0, h), h, 0))
        yield

    half_blocks = blocks // 2

    def query_block(w, d, h):
        cut = slice(h * half_blocks, (h + 1) * half_blocks)
        return q_own[cut] if d == 0 else q_terms[w, cut]

    def query_finish(h, value):
        value = value * grad_factor[None]
        for i in range(half_blocks):
            for r in range(0, BLOCK, rows):
                g = ((h * half_blocks + i) * BLOCK + r) // rows
                dq_ref[0, :, g * HEAD_DIM:(g + 1) * HEAD_DIM] = (
                    value[i, r:r + rows].astype(jnp.bfloat16)
                )

    def build(d, side):
        for s in range(SLOT_DEV):
            slot = ((z + d) % nz * CORES + (core + side) % CORES) * SLOT_DEV + s
            which = 0
            found = 0
            for j in range(MAX_TILES):
                hit = jnp.where((slot_ref[0, j] == slot) & (j < count_ref[0]), 1, 0)
                which = which + hit * j
                found = found + hit
            for kv in range(2):
                block = own[which, kv]
                mine[d, side, s, kv] = jnp.where(found > 0, block, jnp.zeros_like(block))

    def scatter_z():
        for kv in range(2):
            value = terms[kv] * (gate if kv else grad_factor)
            for j in range(MAX_TILES):
                own[j, kv, 0:part, :] = value[tile_rows(j)].astype(jnp.bfloat16)
        order = [nz // 2]
        for t in range(nz // 2 - 1, 0, -1):
            order += [t, nz - t]
        order += [0]
        from_twin = {}
        for d in order:
            build(d, 1)
            from_twin[d] = send(mine.at[d, 1], twin.at[d], other_core)
        for d in order:
            build(d, 0)
        yield

        def prepare(places):
            for d in places:
                from_twin[d].wait_recv()

        def finish(s, value):
            for kv in range(2):
                for t in range(nx):
                    back_out[t, 2 * s + kv, 0:tok, :] = value[kv, t * tok:(t + 1) * tok]

        yield from scatter(
            nz, at_z, lambda w, d, s: mine[d, 0, s] + twin[d, s], z_out, z_in, prepare, finish
        )

    z_half, y_half = nz // 2, ny // 2
    y_ring = gather(ny, at_y, lambda d, h: rowed.at[d, h])
    z_ring = gather_z()
    run(2, y_ring)
    collect()
    run(1, z_ring)
    terms[...] = jnp.zeros(terms.shape, jnp.float32)
    y_steps = 2
    for step in range(z_half):
        if y_steps < 2 * y_half - 2:
            run(1, y_ring)
            y_steps += 1
        run(1, z_ring)
    run(1, z_ring)
    swept = 0
    while y_steps <= 2 * y_half:
        arrived = (y_steps - 2) // 2 if y_steps <= 2 * y_half else y_half
        first_sweep([0] if swept == 0 else [swept, ny - swept])
        swept += 1
        while y_steps <= 2 * y_half and (y_steps - 2) // 2 < swept:
            run(1, y_ring)
            y_steps += 1
    while swept < y_half:
        first_sweep([swept, ny - swept])
        swept += 1
    first_sweep([y_half])

    stat_in[0] = stat_out[0]
    order = sorted(range(1, ny), key=lambda d: -min(d, ny - d))
    for d in order:
        stats[d].wait_recv()
    top = stat_in[0, 0]
    for d in range(1, ny):
        top = jnp.maximum(top, stat_in[d, 0])
    total = jnp.zeros_like(top)
    cross = jnp.zeros_like(top)
    for d in range(ny):
        shrink = jnp.exp2(stat_in[d, 0] - top)
        total = total + stat_in[d, 1] * shrink
        cross = cross + stat_in[d, 2] * shrink
    final[0, 0] = top + jnp.log2(total)
    final[0, 1] = cross / total
    finals = {d: send(final.at[0], final.at[(ny - d) % ny], at_y(d)) for d in order}

    def query_prepare(places):
        for d in places:
            if d != 0:
                finals[(ny - d) % ny].wait_recv()
        if places != [0]:
            second_sweep(places)

    second_sweep([0])
    q_own[...] = q_terms[0]
    y_ring = scatter(ny, at_y, query_block, y_out, y_in, query_prepare, query_finish)
    run(y_half, y_ring)
    z_ring = scatter_z()
    run(3, z_ring)
    run(1, y_ring)
    store = pltpu.make_async_copy(dq_ref, dq_hbm, local_sem.at[0])
    store.start()
    run(z_half, z_ring)

    returns = [send(back_out.at[t], back_in.at[x], at_x(-t)) for t in range(1, nx)]
    back_in[x] = back_out[0]
    for copy in returns:
        copy.wait_recv()
    for h in range(nx):
        for kv, ref in enumerate((dk_ref, dv_ref)):
            both = [
                back_in[h, 2 * s + kv, 0:tok, :].astype(jnp.float32) for s in range(SLOT_DEV)
            ]
            ref[:, :, h * HEAD_DIM:(h + 1) * HEAD_DIM] = (
                jnp.stack(both, axis=1).astype(jnp.bfloat16)
            )
    for copy in started:
        copy.wait_send()
    store.wait()


def on_device(mesh_sizes, queries, out_grad, text_len, image_keys, image_values, tile_counts,
              tile_slots, gate_param):
    nx, ny, nz = mesh_sizes
    tok = image_keys.shape[1]
    rows = queries.shape[1]
    part = nx * tok
    tok_pad = pad16(tok)
    image_keys = jnp.transpose(image_keys, (1, 0, 2))
    image_values = jnp.transpose(image_values, (1, 0, 2))
    pad = pad16(part)
    span = MAX_TILES * part
    blocks = GROUP * rows // BLOCK
    bf16, f32 = jnp.bfloat16, jnp.float32
    vmem = pl.BlockSpec(memory_space=pltpu.VMEM)
    smem = pl.BlockSpec(memory_space=pltpu.SMEM)
    hbm = pl.BlockSpec(memory_space=pl.ANY)
    d = HEAD_DIM
    scratch = [
        (queries.shape, bf16),
        (queries.shape, bf16),
        (image_keys.shape, bf16),
        (image_keys.shape, bf16),
        (queries.shape, bf16),
        ((nx, 2 * SLOT_DEV, tok_pad, d), bf16),
        ((nx, 2 * SLOT_DEV, tok_pad, d), bf16),
        ((nz, CORES, SLOT_DEV, 2, pad, d), bf16),
        ((2, span, d), bf16),
        ((ny, 2, blocks, BLOCK, d), bf16),
        ((ny, 3, blocks, 1, BLOCK), f32),
        ((ny, 3, blocks, 1, BLOCK), f32),
        ((ny, 2, blocks, 1, BLOCK), f32),
        ((2, span, d), f32),
        ((2, blocks, BLOCK, d), f32),
        ((blocks, BLOCK, d), f32),
        ((2, ny // 2, 2, blocks // 2, BLOCK, d), bf16),
        ((2, ny // 2, 2, blocks // 2, BLOCK, d), bf16),
        ((MAX_TILES, 2, pad, d), bf16),
        ((nz, CORES, SLOT_DEV, 2, pad, d), bf16),
        ((nz, SLOT_DEV, 2, pad, d), bf16),
        ((2, nz // 2, SLOT_DEV, 2, pad, d), bf16),
        ((2, nz // 2, SLOT_DEV, 2, pad, d), bf16),
        ((nx, 2 * SLOT_DEV, tok_pad, d), bf16),
        ((nx, 2 * SLOT_DEV, tok_pad, d), bf16),
    ]
    copies = 2 * (nx - 1) + 6 * ny + 6 * nz
    query_grad, key_grad, value_grad = pl.pallas_call(
        functools.partial(kernel, nx, ny, nz),
        out_shape=(
            jax.ShapeDtypeStruct(queries.shape, bf16),
            jax.ShapeDtypeStruct(image_keys.shape, bf16),
            jax.ShapeDtypeStruct(image_values.shape, bf16),
        ),
        in_specs=[hbm, hbm, hbm, hbm, smem, smem, smem, smem],
        out_specs=(hbm, vmem, vmem),
        scratch_shapes=[pltpu.VMEM(shape, dtype) for shape, dtype in scratch] + [
            pltpu.SemaphoreType.DMA((copies,)),
            pltpu.SemaphoreType.DMA((copies,)),
            pltpu.SemaphoreType.DMA((4,)),
        ],
        compiler_params=pltpu.CompilerParams(
            collective_id=0, has_side_effects=True, vmem_limit_bytes=56 * 1024 * 1024
        ),
        name="cross_attention_backward",
    )(queries, out_grad, image_keys, image_values, text_len, tile_counts, tile_slots, gate_param)
    return (
        query_grad, jnp.transpose(key_grad, (1, 0, 2)), jnp.transpose(value_grad, (1, 0, 2))
    )


def solution(mesh):
    sizes = (mesh.shape["head"], mesh.shape["seq"], mesh.shape["img"] // CORES)
    return jax.shard_map(
        functools.partial(on_device, sizes),
        mesh=mesh,
        in_specs=(
            P("img", "seq", "head"),
            P("img", "seq", "head"),
            P("img"),
            P("img", ("seq", "head"), None),
            P("img", ("seq", "head"), None),
            P("img"),
            P("img", None),
            P(),
        ),
        out_specs=(
            P("img", "seq", "head"),
            P("img", ("seq", "head"), None),
            P("img", ("seq", "head"), None),
        ),
        check_vma=False,
    )
```

```python
import functools
import math

import jax
import jax.numpy as jnp
from jax import lax
from jax.experimental import pallas as pl
from jax.experimental.pallas import tpu as pltpu
from jax.sharding import PartitionSpec as P

MESH = pl.DeviceIdType.MESH
HEAD_DIM = 128
MAX_TILES = 4
GROUP = 8
CORES = 2
SLOT_DEV = 2
BLOCK = 512
FAR = 1e30
PIECES = 4


def pad16(n):
    return (n + 15) // 16 * 16


def kernel(
    nx, ny, nz,
    q_hbm, g_hbm, k_hbm, v_hbm, len_ref, count_ref, slot_ref, gate_ref,
    dq_hbm, dk_ref, dv_ref,
    q_ref, g_ref, k_ref, v_ref, dq_ref, head_out, head_in, tiles, keys, rowed,
    stat_out, stat_in, final, terms, q_terms, y_out, y_in, own,
    mine, twin, z_out, z_in, back_out, back_in,
    send_sem, recv_sem, local_sem,
):
    tok = k_ref.shape[0]
    part = nx * tok
    rows = q_ref.shape[1]
    blocks = GROUP * rows // BLOCK
    scale = HEAD_DIM ** -0.5
    img = lax.axis_index("img")
    y = lax.axis_index("seq")
    x = lax.axis_index("head")
    z, core = img // CORES, img % CORES

    def at_z(t):
        return {"img": lax.rem(z + (t + nz), nz) * CORES + core}

    def at_y(t):
        return {"seq": lax.rem(y + (t + ny), ny)}

    def at_x(t):
        return {"head": lax.rem(x + (t + nx), nx)}

    other_core = {"img": z * CORES + (1 - core)}

    loads = []
    for i, (src, dst) in enumerate(
        ((k_hbm, k_ref), (v_hbm, v_ref), (q_hbm, q_ref), (g_hbm, g_ref))
    ):
        loads.append(pltpu.make_async_copy(src, dst, local_sem.at[i]))
        loads[i].start()

    partners = [at_x(t) for t in range(1, nx)] + [other_core]
    partners += [at_y(t) for t in range(1, ny)]
    partners += [at_z(1), at_z(-1)] if nz > 2 else [at_z(1)]
    barrier = pltpu.get_barrier_semaphore()
    for device in partners:
        pl.semaphore_signal(barrier, inc=1, device_id=device, device_id_type=MESH)

    started, returns = [], []

    def send(src, dst, device):
        index = len(started)
        copy = pltpu.make_async_remote_copy(
            src_ref=src, dst_ref=dst, send_sem=send_sem.at[index], recv_sem=recv_sem.at[index],
            device_id=device, device_id_type=MESH,
        )
        copy.start()
        started.append(copy)
        return copy

    def run(steps, ring):
        for _ in range(steps):
            next(ring, None)

    for kv, ref in enumerate((k_ref, v_ref)):
        loads[kv].wait()
        for h in range(nx):
            both = ref[:, :, h * HEAD_DIM:(h + 1) * HEAD_DIM].astype(jnp.float32)
            for s in range(SLOT_DEV):
                head_out[h, 2 * s + kv, 0:tok, :] = both[:, s, :].astype(jnp.bfloat16)
    pl.semaphore_wait(barrier, len(partners))
    arriving = {}
    for t in sorted(range(1, nx), key=lambda t: min(t, nx - t)):
        arriving[t] = send(head_out.at[lax.rem(x + t, nx)], head_in.at[t], at_x(t))

    live = y * rows + lax.broadcasted_iota(jnp.int32, (rows, HEAD_DIM), 0) < len_ref[0]
    loads[2].wait()
    loads[3].wait()
    for g in range(GROUP):
        cut = slice(g * HEAD_DIM, (g + 1) * HEAD_DIM)
        b, r = g * rows // BLOCK, g * rows % BLOCK
        rowed[0, 0, b, r:r + rows, :] = q_ref[0, :, cut]
        rowed[0, 1, b, r:r + rows, :] = jnp.where(
            live, g_ref[0, :, cut], jnp.zeros((rows, HEAD_DIM), jnp.bfloat16)
        )

    def gather(n, at, ref):
        half = n // 2
        copies = {}
        for t in range(1, half + 1):
            for h in range(PIECES):
                for way, step in enumerate((1, -1)):
                    if (way, h) in copies:
                        copies.pop((way, h)).wait_recv()
                    if t < half or h * 2 // PIECES == way:
                        source, target = ref(-step * (t - 1) % n, h), ref(-step * t % n, h)
                        copies[way, h] = send(source, target, at(step))
                yield
        for copy in copies.values():
            copy.wait_recv()
        yield

    def collect():
        for t in range(nx):
            if t > 0:
                arriving[t].wait_recv()
            for q in range(2 * SLOT_DEV):
                block = head_out[x, q, 0:tok, :] if t == 0 else head_in[t, q, 0:tok, :]
                tiles[0, 0, q // 2, q % 2, t * tok:(t + 1) * tok, :] = block

    def gather_z():
        ring = gather(nz, at_z, lambda d, h: tiles.at[d, 0, h // 2, h % 2])
        twins = []

        def forward(d):
            twins.append(send(tiles.at[d, 0], tiles.at[d, 1], other_core))

        for t in range(1, nz // 2 + 1):
            run(PIECES, ring)
            for d in [0] if t == 1 else [t - 1, -(t - 1) % nz]:
                forward(d)
            yield
        next(ring)
        forward(nz // 2)
        yield
        for copy in twins:
            copy.wait_recv()
        for j in range(MAX_TILES):
            slot = jnp.maximum(slot_ref[0, j], 0)
            owner = slot // SLOT_DEV
            step = (owner // CORES + (nz - z)) % nz
            side = (owner + core) % CORES
            for kv in range(2):
                keys[kv, tile_rows(j), :] = tiles[step, side, slot % SLOT_DEV, kv][0:part]
        yield

    bias = [jnp.where(j < count_ref[0], 0.0, FAR).astype(jnp.float32) for j in range(MAX_TILES)]
    to_exp2 = scale * math.log2(math.e)
    by_columns = (((1,), (1,)), ((), ()))

    def scores_of(c, b):
        scores = lax.dot_general(
            keys[0], rowed[c, 0, b], by_columns, preferred_element_type=jnp.float32
        ) * to_exp2
        grads = lax.dot_general(
            keys[1], rowed[c, 1, b], by_columns, preferred_element_type=jnp.float32
        )
        return scores, grads

    def tile_rows(j):
        return slice(j * part, (j + 1) * part)

    def over(chunks, body):
        def step(i, carry):
            if len(chunks) == 1:
                body(chunks[0], 0, i)
            else:
                body(jnp.where(i < blocks, chunks[0], chunks[1]), i // blocks, i % blocks)
            return carry

        lax.fori_loop(0, len(chunks) * blocks, step, 0)

    stats = {}

    def first_sweep(chunks):
        def body(c, w, b):
            scores, grads = scores_of(c, b)
            top = jnp.full((1, BLOCK), -FAR, jnp.float32)
            for j in range(MAX_TILES):
                highest = jnp.max(scores[tile_rows(j)], axis=0, keepdims=True)
                top = jnp.maximum(top, highest - bias[j])
            total = jnp.zeros((1, BLOCK), jnp.float32)
            cross = jnp.zeros((1, BLOCK), jnp.float32)
            for j in range(MAX_TILES):
                e = jnp.exp2(scores[tile_rows(j)] - (top + bias[j]))
                total = total + jnp.sum(e, axis=0, keepdims=True)
                cross = cross + jnp.sum(e * grads[tile_rows(j)], axis=0, keepdims=True)
            stat_out[c, 0, b] = top
            stat_out[c, 1, b] = total
            stat_out[c, 2, b] = cross

        over(chunks, body)
        for d in chunks:
            if d != 0:
                stats[d] = send(stat_out.at[d], stat_in.at[(ny - d) % ny], at_y(d))

    gate = jnp.tanh(jnp.full((8, HEAD_DIM), gate_ref[0], jnp.float32))[0:1]
    grad_factor = gate * scale

    def second_sweep(chunks):
        def body(c, w, b):
            scores, grads = scores_of(c, b)
            top, delta = final[c, 0, b], final[c, 1, b]
            weights, score_grads = [], []
            for j in range(MAX_TILES):
                e = jnp.exp2(scores[tile_rows(j)] - (top + bias[j]))
                weights.append(e)
                score_grads.append(e * (grads[tile_rows(j)] - delta))
            weights = jnp.concatenate(weights, axis=0).astype(jnp.bfloat16)
            score_grads = jnp.concatenate(score_grads, axis=0).astype(jnp.bfloat16)
            terms[0] += jnp.dot(score_grads, rowed[c, 0, b], preferred_element_type=jnp.float32)
            terms[1] += jnp.dot(weights, rowed[c, 1, b], preferred_element_type=jnp.float32)
            q_terms[c, b] = lax.dot_general(
                score_grads, keys[0], (((0,), (0,)), ((), ())),
                preferred_element_type=jnp.float32,
            )

        over(chunks, body)

    def scatter(n, pieces, at, block, out, arrived, prepare, finish):
        half = n // 2
        copies = {}

        def total(value, h, step):
            for way in range(2) if step == 0 else [0 if step > 0 else 1]:
                if (way, h) in copies:
                    copies.pop((way, h)).wait_recv()
                    value = value + arrived[way, half - abs(step) - 1, h]
            return value

        for s in range(half):
            t = half - s
            prepare([half] if s == 0 else [t, n - t])
            for h in range(pieces):
                for way, step in enumerate((1, -1)):
                    if s == 0 and h * 2 // pieces != way:
                        continue
                    value = block(way if s > 0 else 0, step * t % n, h)
                    place = (way, s, h)
                    out[place] = total(value, h, step * t).astype(out.dtype)
                    copies[way, h] = send(out.at[place], arrived.at[place], at(step))
            yield
        prepare([0])
        for h in range(pieces):
            finish(h, total(block(0, 0, h), h, 0))
        yield

    def query_block(w, d, h):
        return q_terms[d, h]

    def query_finish(h, value):
        value = value * grad_factor
        for r in range(0, BLOCK, rows):
            g = (h * BLOCK + r) // rows
            dq_ref[0, :, g * HEAD_DIM:(g + 1) * HEAD_DIM] = value[r:r + rows].astype(jnp.bfloat16)

    def build(d, side):
        for s in range(SLOT_DEV):
            slot = ((z + d) % nz * CORES + (core + side) % CORES) * SLOT_DEV + s
            which = 0
            found = 0
            for j in range(MAX_TILES):
                hit = jnp.where((slot_ref[0, j] == slot) & (j < count_ref[0]), 1, 0)
                which = which + hit * j
                found = found + hit
            for kv in range(2):
                block = own[which, kv]
                mine[d, side, s, kv] = jnp.where(found > 0, block, jnp.zeros_like(block))

    def scatter_z():
        for kv in range(2):
            value = terms[kv] * (gate if kv else grad_factor)
            for j in range(MAX_TILES):
                own[j, kv, 0:part, :] = value[tile_rows(j)].astype(jnp.bfloat16)
        order = [nz // 2]
        for t in range(nz // 2 - 1, 0, -1):
            order += [t, nz - t]
        order += [0]
        from_twin = {}
        for d in order:
            build(d, 1)
            from_twin[d] = send(mine.at[d, 1], twin.at[d], other_core)
        for d in order:
            build(d, 0)
        yield

        def prepare(places):
            for d in places:
                from_twin[d].wait_recv()

        def finish(h, value):
            back_in[x, h, 0:tok, :] = value[0:tok]
            for t in range(1, nx):
                back_out[t, h, 0:tok, :] = value[t * tok:(t + 1) * tok]
                returns.append(send(back_out.at[t, h], back_in.at[x, h], at_x(-t)))

        def block(w, d, h):
            return mine[d, 0, h // 2, h % 2] + twin[d, h // 2, h % 2]

        yield from scatter(nz, PIECES, at_z, block, z_out, z_in, prepare, finish)

    z_half, y_half = nz // 2, ny // 2
    part_blocks = blocks // 2
    y_ring = gather(
        ny, at_y, lambda d, h: rowed.at[d, h // 2, pl.ds(h % 2 * part_blocks, part_blocks)]
    )
    z_ring = gather_z()
    run(PIECES, y_ring)
    collect()
    run(1, z_ring)
    terms[...] = jnp.zeros(terms.shape, jnp.float32)
    for step in range(z_half):
        run(PIECES // 2, y_ring)
        run(1, z_ring)
    passed = PIECES + z_half * PIECES // 2
    if y_half > 2:
        run(1, y_ring)
        passed += 1
    run(1, z_ring)
    first_sweep([0])
    for step in range(1, y_half):
        missing = (step + 1) * PIECES - passed
        ahead = 2 if step < y_half - 1 else PIECES
        steps = max(missing, min(ahead, y_half * PIECES - passed))
        run(steps, y_ring)
        passed += steps
        first_sweep([step, ny - step])
    run(y_half * PIECES + 1 - passed, y_ring)
    first_sweep([y_half])

    stat_in[0] = stat_out[0]
    order = sorted(range(1, ny), key=lambda d: -min(d, ny - d))
    for d in order:
        stats[d].wait_recv()
    top = stat_in[0, 0]
    for d in range(1, ny):
        top = jnp.maximum(top, stat_in[d, 0])
    total = jnp.zeros_like(top)
    cross = jnp.zeros_like(top)
    for d in range(ny):
        shrink = jnp.exp2(stat_in[d, 0] - top)
        total = total + stat_in[d, 1] * shrink
        cross = cross + stat_in[d, 2] * shrink
    final[0, 0] = top + jnp.log2(total)
    final[0, 1] = cross / total
    finals = {d: send(final.at[0], final.at[(ny - d) % ny], at_y(d)) for d in order}

    def sweep_all(chunks):
        for d in chunks:
            if d != 0:
                finals[(ny - d) % ny].wait_recv()
        second_sweep(chunks)

    z_ring = scatter_z()
    y_ring = scatter(
        ny, blocks, at_y, query_block, y_out, y_in, lambda places: None, query_finish
    )
    sweep_all([0])
    sweep_all([y_half])
    run(1, y_ring)
    y_steps = 1
    for t in range(y_half - 1, 0, -1):
        sweep_all([t, ny - t])
        if t == 2:
            run(1, y_ring)
            y_steps += 1
    run(1, z_ring)
    run(1, y_ring)
    run(2, z_ring)
    y_steps += 1
    run(y_half - y_steps, y_ring)
    run(max(z_half - 2, 0), z_ring)
    run(2, y_ring)
    store = pltpu.make_async_copy(dq_ref, dq_hbm, local_sem.at[0])
    store.start()
    run(z_half, z_ring)
    for copy in returns:
        copy.wait_recv()
    for h in range(nx):
        for kv, ref in enumerate((dk_ref, dv_ref)):
            both = [
                back_in[h, 2 * s + kv, 0:tok, :].astype(jnp.float32) for s in range(SLOT_DEV)
            ]
            ref[:, :, h * HEAD_DIM:(h + 1) * HEAD_DIM] = (
                jnp.stack(both, axis=1).astype(jnp.bfloat16)
            )
    for copy in started:
        copy.wait_send()
    store.wait()


def on_device(mesh_sizes, queries, out_grad, text_len, image_keys, image_values, tile_counts,
              tile_slots, gate_param):
    nx, ny, nz = mesh_sizes
    tok = image_keys.shape[1]
    rows = queries.shape[1]
    part = nx * tok
    tok_pad = pad16(tok)
    image_keys = jnp.transpose(image_keys, (1, 0, 2))
    image_values = jnp.transpose(image_values, (1, 0, 2))
    pad = pad16(part)
    span = MAX_TILES * part
    blocks = GROUP * rows // BLOCK
    bf16, f32 = jnp.bfloat16, jnp.float32
    vmem = pl.BlockSpec(memory_space=pltpu.VMEM)
    smem = pl.BlockSpec(memory_space=pltpu.SMEM)
    hbm = pl.BlockSpec(memory_space=pl.ANY)
    d = HEAD_DIM
    scratch = [
        (queries.shape, bf16),
        (queries.shape, bf16),
        (image_keys.shape, bf16),
        (image_keys.shape, bf16),
        (queries.shape, bf16),
        ((nx, 2 * SLOT_DEV, tok_pad, d), bf16),
        ((nx, 2 * SLOT_DEV, tok_pad, d), bf16),
        ((nz, CORES, SLOT_DEV, 2, pad, d), bf16),
        ((2, span, d), bf16),
        ((ny, 2, blocks, BLOCK, d), bf16),
        ((ny, 3, blocks, 1, BLOCK), f32),
        ((ny, 3, blocks, 1, BLOCK), f32),
        ((ny, 2, blocks, 1, BLOCK), f32),
        ((2, span, d), f32),
        ((ny, blocks, BLOCK, d), f32),
        ((2, ny // 2, blocks, BLOCK, d), bf16),
        ((2, ny // 2, blocks, BLOCK, d), bf16),
        ((MAX_TILES, 2, pad, d), bf16),
        ((nz, CORES, SLOT_DEV, 2, pad, d), bf16),
        ((nz, SLOT_DEV, 2, pad, d), bf16),
        ((2, nz // 2, PIECES, pad, d), bf16),
        ((2, nz // 2, PIECES, pad, d), bf16),
        ((nx, 2 * SLOT_DEV, tok_pad, d), bf16),
        ((nx, 2 * SLOT_DEV, tok_pad, d), bf16),
    ]
    copies = (PIECES + 1) * (nx - 1) + 2 * (PIECES + 1) * (ny + nz)
    query_grad, key_grad, value_grad = pl.pallas_call(
        functools.partial(kernel, nx, ny, nz),
        out_shape=(
            jax.ShapeDtypeStruct(queries.shape, bf16),
            jax.ShapeDtypeStruct(image_keys.shape, bf16),
            jax.ShapeDtypeStruct(image_values.shape, bf16),
        ),
        in_specs=[hbm, hbm, hbm, hbm, smem, smem, smem, smem],
        out_specs=(hbm, vmem, vmem),
        scratch_shapes=[pltpu.VMEM(shape, dtype) for shape, dtype in scratch] + [
            pltpu.SemaphoreType.DMA((copies,)),
            pltpu.SemaphoreType.DMA((copies,)),
            pltpu.SemaphoreType.DMA((4,)),
        ],
        compiler_params=pltpu.CompilerParams(
            collective_id=0, has_side_effects=True, vmem_limit_bytes=56 * 1024 * 1024
        ),
        name="cross_attention_backward",
    )(queries, out_grad, image_keys, image_values, text_len, tile_counts, tile_slots, gate_param)
    return (
        query_grad, jnp.transpose(key_grad, (1, 0, 2)), jnp.transpose(value_grad, (1, 0, 2))
    )


def solution(mesh):
    sizes = (mesh.shape["head"], mesh.shape["seq"], mesh.shape["img"] // CORES)
    return jax.shard_map(
        functools.partial(on_device, sizes),
        mesh=mesh,
        in_specs=(
            P("img", "seq", "head"),
            P("img", "seq", "head"),
            P("img"),
            P("img", ("seq", "head"), None),
            P("img", ("seq", "head"), None),
            P("img"),
            P("img", None),
            P(),
        ),
        out_specs=(
            P("img", "seq", "head"),
            P("img", ("seq", "head"), None),
            P("img", ("seq", "head"), None),
        ),
        check_vma=False,
    )
```
